32 devices in a mesh: tm: 8 (over y, x, core), head: 4 (over z).
Axes of the slice: x: 2, y: 2, z: 4, core: 2. Of those that a mesh axis runs over, the one named last changes fastest.
Arguments:
- queries: bfloat16 [4096, 1024], P('tm', 'head'), may hold values from -5.5 to 5.5
- key_states: bfloat16 [4096, 1024], P('tm', 'head'), may hold values from -5.5 to 5.5
- value_states: bfloat16 [4096, 1024], P('tm', 'head'), may hold values from -6 to 6
- out_weight: bfloat16 [1024, 1024], P('head'), may hold values from -6 to 6
- upstream: bfloat16 [4096, 1024], P('tm'), may hold values from -6 to 6
- windows: int32 [16], P('head'), may hold values from 64 to 256, as said below
- offsets: int32 [16], P('head'), may hold values from 0 to 7
Outputs:
- mixed: bfloat16 [4096, 1024], P('tm')
- grad_queries: bfloat16 [4096, 1024], P('tm', 'head')
- grad_keys: bfloat16 [4096, 1024], P('tm', 'head')
- grad_values: bfloat16 [4096, 1024], P('tm', 'head')
The draws below stay inside these ranges and needn't reach their ends.
Inputs may be any that keep to these rules, and one draw needn't show every extreme that they name: `windows`: each head's window reaches at most 256 positions to each side, and some head's window is exactly 256.
All inputs are finite; a program needn't handle non-finite values.
Results may differ from the reference program's by a relative error of at most 0.017.
Values may be sent and summed in bfloat16 or wider, within the bound.
A program may use at most 128 MiB of HBM per device.

```python
import math
import jax
import jax.numpy as jnp
from jax import lax

HEADS = 16
HEAD_DIM = 64
D = 1024
TOK_DEV = 512
TOKENS = 4096
WIN = 256
LEVELS = 3
N_TM = 8


def base_draw(key):
    return jnp.clip(jax.random.normal(key, (TOKENS, D), jnp.float32), -5.5, 5.5)


def draw_queries(key, part):
    values = base_draw(jax.random.fold_in(key, 11))
    return values.astype(jnp.bfloat16)


def draw_key_states(key, part):
    values = base_draw(jax.random.fold_in(key, 12))
    return values.astype(jnp.bfloat16)


def draw_windows(key, part):
    spans = jax.random.randint(jax.random.fold_in(key, 21), (HEADS,), WIN // 4, WIN + 1)
    chosen = jax.random.randint(jax.random.fold_in(key, 22), (), 0, HEADS)
    return jnp.where(jnp.arange(HEADS) == chosen, WIN, spans).astype(jnp.int32)


def touch_ends(result, own_key, least, high):
    longest = result.shape.index(max(result.shape))
    spots = []
    for shift in (0, 1):
        where = [jax.random.randint(jax.random.fold_in(own_key, axis), (), 0, length) for axis, length in enumerate(result.shape)]
        where[longest] = (where[longest] + shift) % result.shape[longest]
        spots.append(tuple(where))
    return result.at[spots[0]].set(least).at[spots[1]].set(high)


def level_of(key, shape, shards, smallest, largest):
    level, own = 1.0, jax.random.fold_in(key, 6)
    for axis_at, blocks in shards:
        heights = jnp.exp(jax.random.uniform(jax.random.fold_in(own, axis_at), (blocks,), jnp.float32, smallest / len(shards), largest / len(shards)))
        level = level * jnp.repeat(heights, shape[axis_at] // blocks).reshape([-1 if axis == axis_at else 1 for axis in range(len(shape))])
    return level


def normal_values(stream_key, dims, deviation, most, cuts=(), kind=jnp.bfloat16):
    values = deviation * jax.random.normal(stream_key, dims, jnp.float32)
    if cuts:
        values = values * level_of(stream_key, dims, cuts, -0.22, 0.18)
    return jnp.clip(values, -most, most).astype(kind)


def setup_inputs(seed: int = 0) -> dict:
    key_list = jax.random.split(jax.random.key(seed), 8)
    queries = draw_queries(jax.random.fold_in(key_list[7], 71), 0)
    key_states = draw_key_states(jax.random.fold_in(key_list[7], 71), 0)
    value_states = normal_values(key_list[2], (TOKENS, D), 1.0, 6.0, ((0, 8), (1, 4)))
    out_weight = normal_values(key_list[3], (D, D), 1.0, 6.0, ((0, 4),))
    upstream = normal_values(key_list[4], (TOKENS, D), 1.0, 6.0, ((0, 8),))
    windows = draw_windows(jax.random.fold_in(key_list[7], 71), 0)
    offsets = touch_ends(jax.random.randint(key_list[6], (HEADS,), 0, N_TM), jax.random.fold_in(key_list[6], 1), 0, N_TM - 1).astype(jnp.int32)
    return dict(queries=queries, key_states=key_states, value_states=value_states, out_weight=out_weight, upstream=upstream, windows=windows, offsets=offsets)


HIGH = lax.Precision.HIGHEST

def lane_select(grouped, lane_hit):
    lane_mask = lane_hit.reshape(lane_hit.shape + (1,) * (grouped.ndim - 3))
    return lax.optimization_barrier(jnp.sum(jnp.where(lane_mask[None], grouped, jnp.zeros((), grouped.dtype)), axis=1))

def lane_spread(values, lane_hit, filler):
    lane_mask = lane_hit.reshape(lane_hit.shape + (1,) * (values.ndim - 2))
    spread = jnp.where(lane_mask[None], values[:, None], filler)
    return spread.reshape((-1,) + values.shape[1:])

def attend_block(query_block, key_block, value_block, allowed, score_scale):
    scores = jnp.einsum('qhd,khd->hqk', query_block, key_block, precision=HIGH) * score_scale
    scores = jnp.where(allowed, scores, -jnp.inf)
    block_max = lax.optimization_barrier(jnp.max(scores, axis=2))
    weights = jnp.exp(scores - block_max[:, :, None])
    block_sum = lax.optimization_barrier(jnp.sum(weights, axis=2))
    rounded = lax.optimization_barrier(weights.astype(jnp.bfloat16)).astype(jnp.float32)
    block_acc = jnp.einsum('hqk,khd->qhd', rounded, value_block, precision=HIGH)
    return (block_max.T, block_sum.T, block_acc)

def back_block(query_block, key_block, value_block, grad_block, norm_block, delta_block, allowed, score_scale):
    scores = jnp.einsum('qhd,khd->hqk', query_block, key_block, precision=HIGH) * score_scale
    scores = jnp.where(allowed, scores, -jnp.inf)
    probs = jnp.exp(scores - norm_block.T[:, :, None])
    dots = jnp.einsum('qhd,khd->hqk', grad_block, value_block, precision=HIGH)
    score_grad = lax.optimization_barrier((probs * (dots - delta_block.T[:, :, None])).astype(jnp.bfloat16)).astype(jnp.float32)
    prob_round = lax.optimization_barrier(probs.astype(jnp.bfloat16)).astype(jnp.float32)
    query_grad = jnp.einsum('hqk,khd->qhd', score_grad, key_block, precision=HIGH) * score_scale
    key_grad = jnp.einsum('hqk,qhd->khd', score_grad, query_block, precision=HIGH) * score_scale
    value_grad = jnp.einsum('hqk,qhd->khd', prob_round, grad_block, precision=HIGH)
    return (query_grad, key_grad, value_grad)

def merge_stats(running, extra):
    new_max = jnp.maximum(running[0], extra[0])
    old_scale = jnp.exp(running[0] - new_max)
    new_scale = jnp.exp(extra[0] - new_max)
    return (new_max, running[1] * old_scale + extra[1] * new_scale, running[2] * old_scale[:, :, None] + extra[2] * new_scale[:, :, None])

def reference(queries, key_states, value_states, out_weight, upstream, windows, offsets):
    seq_total = TOKENS
    score_scale = 1.0 / math.sqrt(HEAD_DIM)
    half_width = WIN
    block_rows = min(512, TOK_DEV)
    span_rows = block_rows + 2 * half_width
    heads_shape = (seq_total, HEADS, HEAD_DIM)
    query_f = queries.astype(jnp.float32).reshape(heads_shape)
    key_f = key_states.astype(jnp.float32).reshape(heads_shape)
    value_f = value_states.astype(jnp.float32).reshape(heads_shape)
    pad_spec = ((half_width, half_width), (0, 0), (0, 0))
    key_pad = jnp.pad(key_f, pad_spec)
    value_pad = jnp.pad(value_f, pad_spec)
    block_starts = (jnp.arange(seq_total // block_rows) * block_rows).astype(jnp.int32)

    def window_allowed(start):
        query_pos = start + jnp.arange(block_rows)[:, None]
        key_pos = start - half_width + jnp.arange(span_rows)[None, :]
        inside = (key_pos >= 0) & (key_pos < seq_total)
        near = jnp.abs(query_pos - key_pos)[None] <= windows[:, None, None]
        return near & inside[None]

    def window_forward(start):
        return attend_block(lax.dynamic_slice_in_dim(query_f, start, block_rows, 0), lax.dynamic_slice_in_dim(key_pad, start, span_rows, 0), lax.dynamic_slice_in_dim(value_pad, start, span_rows, 0), window_allowed(start), score_scale)
    win_max, win_sum, win_acc = lax.map(window_forward, block_starts)
    running = (win_max.reshape(seq_total, HEADS), win_sum.reshape(seq_total, HEADS), win_acc.reshape(heads_shape))
    level_info = []
    for level_no in range(1, LEVELS + 1):
        level_rate = 2 ** level_no
        seg_count = seq_total // (level_rate * TOK_DEV)
        lane_hit = jnp.arange(level_rate)[:, None] == (offsets % level_rate)[None, :]

        def select_lanes(array):
            grouped = array.reshape((seq_total // level_rate, level_rate) + array.shape[1:])
            return lane_select(grouped, lane_hit).reshape((seg_count, TOK_DEV) + array.shape[1:])
        level_q = select_lanes(query_f)
        level_k = select_lanes(key_f)
        level_v = select_lanes(value_f)

        def level_forward(inputs):
            return attend_block(inputs[0], inputs[1], inputs[2], True, score_scale)
        level_max, level_sum, level_acc = lax.map(level_forward, (level_q, level_k, level_v))
        extra = (lane_spread(level_max.reshape(-1, HEADS), lane_hit, -jnp.inf), lane_spread(level_sum.reshape(-1, HEADS), lane_hit, 0.0), lane_spread(level_acc.reshape(-1, HEADS, HEAD_DIM), lane_hit, 0.0))
        running = merge_stats(running, extra)
        level_info.append((level_rate, seg_count, lane_hit, level_q, level_k, level_v))
    run_max, run_sum, run_acc = running
    attn = (run_acc / run_sum[:, :, None]).astype(jnp.bfloat16)
    log_norm = run_max + jnp.log(run_sum)
    mixed = jnp.dot(attn.reshape(seq_total, D), out_weight, preferred_element_type=jnp.float32).astype(jnp.bfloat16)
    grad_attn = jnp.dot(upstream, out_weight.T, preferred_element_type=jnp.float32).astype(jnp.bfloat16)
    grad_f = grad_attn.astype(jnp.float32).reshape(heads_shape)
    row_delta = lax.optimization_barrier(jnp.sum(grad_f * attn.astype(jnp.float32), axis=2))

    def window_backward(carry, start):
        key_acc, value_acc = carry
        query_grad, key_grad, value_grad = back_block(lax.dynamic_slice_in_dim(query_f, start, block_rows, 0), lax.dynamic_slice_in_dim(key_pad, start, span_rows, 0), lax.dynamic_slice_in_dim(value_pad, start, span_rows, 0), lax.dynamic_slice_in_dim(grad_f, start, block_rows, 0), lax.dynamic_slice_in_dim(log_norm, start, block_rows, 0), lax.dynamic_slice_in_dim(row_delta, start, block_rows, 0), window_allowed(start), score_scale)
        key_acc = lax.dynamic_update_slice_in_dim(key_acc, lax.dynamic_slice_in_dim(key_acc, start, span_rows, 0) + key_grad, start, 0)
        value_acc = lax.dynamic_update_slice_in_dim(value_acc, lax.dynamic_slice_in_dim(value_acc, start, span_rows, 0) + value_grad, start, 0)
        return ((key_acc, value_acc), query_grad)
    zero_pad = jnp.zeros(key_pad.shape, jnp.float32)
    (key_acc, value_acc), query_parts = lax.scan(window_backward, (zero_pad, zero_pad), block_starts)
    query_total = query_parts.reshape(heads_shape)
    key_total = key_acc[half_width:half_width + seq_total]
    value_total = value_acc[half_width:half_width + seq_total]
    for level_rate, seg_count, lane_hit, level_q, level_k, level_v in level_info:

        def select_lanes(array):
            grouped = array.reshape((seq_total // level_rate, level_rate) + array.shape[1:])
            return lane_select(grouped, lane_hit).reshape((seg_count, TOK_DEV) + array.shape[1:])

        def level_backward(inputs):
            return back_block(inputs[0], inputs[1], inputs[2], inputs[3], inputs[4], inputs[5], True, score_scale)
        query_grad, key_grad, value_grad = lax.map(level_backward, (level_q, level_k, level_v, select_lanes(grad_f), select_lanes(log_norm), select_lanes(row_delta)))
        query_total = query_total + lane_spread(query_grad.reshape(-1, HEADS, HEAD_DIM), lane_hit, 0.0)
        key_total = key_total + lane_spread(key_grad.reshape(-1, HEADS, HEAD_DIM), lane_hit, 0.0)
        value_total = value_total + lane_spread(value_grad.reshape(-1, HEADS, HEAD_DIM), lane_hit, 0.0)
    return (mixed, query_total.reshape(seq_total, D).astype(jnp.bfloat16), key_total.reshape(seq_total, D).astype(jnp.bfloat16), value_total.reshape(seq_total, D).astype(jnp.bfloat16))
```

```python
import functools
import math

import jax
import jax.numpy as jnp
from jax import lax
from jax.experimental import pallas as pl
from jax.experimental.pallas import tpu as pltpu
from jax.sharding import PartitionSpec as P

MESH = pl.DeviceIdType.MESH
F32 = jnp.float32
BF16 = jnp.bfloat16
NEG = -1e30


def nt(a, b):
    return lax.dot_general(a, b, (((1,), (1,)), ((), ())), preferred_element_type=F32)


def nn(a, b):
    return lax.dot_general(a, b, (((1,), (0,)), ((), ())), preferred_element_type=F32)


def flipped(me, x):
    peer = me
    for k in range(x.bit_length()):
        if x >> k & 1:
            peer = peer + (1 - 2 * (me // 2**k % 2)) * 2**k
    return peer


def kernel(
    tm, nz, heads,
    q_ref, k_ref, v_ref, w_ref, up_ref, win_ref, off_ref,
    dq_ref, dk_ref, dv_ref, attn_ref,
    order, back, q4, g4, gt, kvnat, kvown, nkv, pkv, ownt, nt_kv, pt_kv,
    cown, cp1, cp2, top, total, delta, ot, dqt,
    accn, accp, acco, sendn, sendp, gotn, gotp, attng, send_sem, recv_sem,
):
    rows, width = q_ref.shape
    dim = width // heads
    levels = tm.bit_length() - 1
    half = rows // 2
    slab = rows // tm
    quarter = rows // 4
    scale = 1.0 / math.sqrt(dim)
    me = lax.axis_index("tm")
    zi = lax.axis_index("head")
    right = (me + 1) % tm
    left = (me + tm - 1) % tm

    barrier = pltpu.get_barrier_semaphore()
    for x in range(1, tm):
        pl.semaphore_signal(
            barrier, inc=1, device_id=((me + x) % tm, zi), device_id_type=MESH
        )
    for x in range(1, nz):
        pl.semaphore_signal(
            barrier, inc=1, device_id=(me, (zi + x) % nz), device_id_type=MESH
        )

    def count_of(x):
        return rows >> x.bit_length()

    def slot_of(x):
        m = x.bit_length()
        return (m - 1) * half + (x - 2 ** (m - 1)) * (rows >> m)

    def remote(src, dst, sem, device):
        return pltpu.make_async_remote_copy(
            src_ref=src, dst_ref=dst, send_sem=send_sem.at[sem], recv_sem=recv_sem.at[sem],
            device_id=device, device_id_type=MESH,
        )

    kvnat[:, :width] = k_ref[...]
    kvnat[:, width:] = v_ref[...]
    pl.semaphore_wait(barrier, tm + nz - 2)
    near = [
        remote(kvnat.at[pl.ds(half, half)], nkv.at[pl.ds(0, half)], 0, (right, zi)),
        remote(kvnat.at[pl.ds(0, half)], nkv.at[pl.ds(half, half)], 1, (left, zi)),
    ]
    for copy in near:
        copy.start()

    def reversed_bits(s):
        out = jnp.zeros_like(s)
        for k in range(levels):
            out = out + ((s >> k) & 1) * 2 ** (levels - 1 - k)
        return out

    def place(row):
        return (row % slab) * tm + reversed_bits(row // slab)

    iota = lambda shape, axis: lax.broadcasted_iota(jnp.int32, shape, axis)
    place_col = place(iota((rows, 1), 0))
    place_row = place(iota((1, rows), 1))
    order[...] = jnp.where(iota((rows, rows), 1) == place_col, 1.0, 0.0).astype(BF16)
    back[...] = jnp.where(iota((rows, rows), 0) == place_row, 1.0, 0.0).astype(BF16)

    def off_cols(cols):
        head = (iota((1, cols), 1) % width) // dim
        out = jnp.zeros((1, cols), jnp.int32)
        for h in range(heads):
            out = jnp.where(head == h, off_ref[h], out)
        return out

    def swapped(x):
        off = off_cols(x.shape[1])
        for k in range(levels):
            size = slab * 2 ** (levels - 1 - k)
            other = jnp.concatenate(
                [x[(i ^ 1) * size : (i ^ 1) * size + size] for i in range(rows // size)], 0
            )
            x = jnp.where(((off >> k) & 1) == 1, other, x)
        return x

    def to_order(x):
        return swapped(nn(order[...], x))

    def from_order(x):
        return nn(back[...], swapped(x).astype(BF16))

    kvp = to_order(kvnat[...])
    kvown[...] = kvp.astype(BF16)
    far = [
        remote(
            kvown.at[pl.ds(0, count_of(x))], pkv.at[pl.ds(slot_of(x), count_of(x))], 1 + x,
            (flipped(me, x), zi),
        )
        for x in range(1, tm)
    ]
    for copy in far:
        copy.start()
    ownt[...] = jnp.transpose(kvp).astype(BF16)
    col_head = iota((1, width), 1) // dim
    qp = to_order(q_ref[...]) * scale
    grad = nt(up_ref[...], w_ref[...]).astype(BF16)
    gp = to_order(grad)
    gt[...] = jnp.transpose(gp)
    for h in range(heads):
        at = pl.ds(h * rows, rows)
        q4[at, :] = jnp.where(col_head == h, qp, 0.0).astype(BF16)
        g4[at, :] = jnp.where(col_head == h, gp, 0.0).astype(BF16)

    def shared(i, j, first):
        out = jnp.zeros(jnp.broadcast_shapes(i.shape, j.shape), F32)
        for l in range(first, levels + 1):
            out = out + jnp.where(jnp.maximum(i, j) < (rows >> l), 1.0, 0.0)
        return out

    cown[...] = shared(iota((1, rows), 1), iota((rows, 1), 0), 1)
    cp1[...] = shared(iota((1, half), 1), iota((half, 1), 0), 1)
    for m in range(2, levels + 1):
        cp2[pl.ds((m - 2) * half, half), :] = shared(
            iota((1, quarter), 1), iota((half, 1), 0) % (rows >> m), m
        )

    near_row = iota((rows, 1), 0)
    gap = 8 * rows
    pos_near = jnp.where(
        near_row < half,
        jnp.where(me > 0, near_row - half, -gap),
        jnp.where(me < tm - 1, near_row + half, gap),
    )

    def own_count(h):
        off = off_ref[h] % tm
        d = (place_col ^ off) - (place_row ^ off)
        return cown[...] + jnp.where(jnp.abs(d) <= win_ref[h], 1.0, 0.0)

    def near_hit(h):
        off = off_ref[h] % tm
        return jnp.abs(pos_near - (place_row ^ off)) <= win_ref[h]

    def sum0(x):
        return jnp.sum(x, axis=0, keepdims=True)

    def max0(x):
        return jnp.max(x, axis=0, keepdims=True)

    def head_rows(h, count):
        return pl.ds(pl.multiple_of(h * rows, rows), count)

    def feat(h):
        return pl.ds(pl.multiple_of(h * dim, dim), dim)

    def vfeat(h):
        return pl.ds(pl.multiple_of(width + h * dim, dim), dim)

    def own_forward(h, _):
        s = nt(kvown[:, :width], q4[head_rows(h, rows), :])
        c = own_count(h)
        s = jnp.where(c > 0.0, s, NEG)
        m = max0(s)
        p = c * jnp.exp(s - m)
        top[h] = m
        total[h] = sum0(p)
        ot[feat(h), :] = nn(ownt[vfeat(h), :], p.astype(BF16))
        return 0

    lax.fori_loop(0, heads, own_forward, 0)

    for copy in near + far:
        copy.wait()
    nt_kv[...] = jnp.transpose(nkv[...].astype(F32)).astype(BF16)
    pt_kv[...] = jnp.transpose(pkv[...].astype(F32)).astype(BF16)

    def widen(a, fill):
        missing = rows - a.shape[1]
        return jnp.concatenate([a, jnp.full((a.shape[0], missing), fill, F32)], 1)

    def other_forward(h, _):
        sn = nt(nkv[:, :width], q4[head_rows(h, rows), :])
        s1 = nt(pkv[:half, :width], q4[head_rows(h, half), :])
        s2 = nt(pkv[half:, :width], q4[head_rows(h, quarter), :])
        sn = jnp.where(near_hit(h), sn, NEG)
        c2 = cp2[...]
        s2 = jnp.where(c2 > 0.0, s2, NEG)
        m0 = top[h]
        m = jnp.maximum(
            jnp.maximum(m0, max0(sn)),
            jnp.maximum(widen(max0(s1), NEG), widen(max0(s2), NEG)),
        )
        pn = jnp.exp(sn - m)
        p1 = cp1[...] * jnp.exp(s1 - m[:, :half])
        p2 = c2 * jnp.exp(s2 - m[:, :quarter])
        keep = jnp.exp(m0 - m)
        l = total[h] * keep + sum0(pn) + widen(sum0(p1), 0.0) + widen(sum0(p2), 0.0)
        o = ot[feat(h), :] * keep + nn(nt_kv[vfeat(h), :], pn.astype(BF16))
        o = o + widen(nn(pt_kv[vfeat(h), :half], p1.astype(BF16)), 0.0)
        o = o + widen(nn(pt_kv[vfeat(h), half:], p2.astype(BF16)), 0.0)
        o = (o / l).astype(BF16).astype(F32)
        ot[feat(h), :] = o
        top[h] = m + jnp.log(l)
        delta[h] = sum0(o * gt[feat(h), :])
        return 0

    lax.fori_loop(0, heads, other_forward, 0)

    attng[zi] = from_order(jnp.transpose(ot[...])).astype(BF16)
    spread = [
        remote(attng.at[zi], attng.at[zi], 2 * tm + 1 + x, (me, (zi + x) % nz))
        for x in range(1, nz)
    ]
    for copy in spread:
        copy.start()

    accn[...] = jnp.zeros_like(accn)
    accp[...] = jnp.zeros_like(accp)
    acco[...] = jnp.zeros_like(acco)

    def back_part(h, kv, at, kt, queries, s_of, c_of):
        q = q4[head_rows(h, queries), :]
        g = g4[head_rows(h, queries), :]
        s = s_of(nt(kv[at, :width], q))
        p = jnp.exp(s - top[h][:, :queries])
        p = c_of(p)
        dots = nt(kv[at, width:], g)
        ds = (p * (dots - delta[h][:, :queries])).astype(BF16)
        return nn(ds, q), nn(p.astype(BF16), g), nn(kt, ds)

    def other_backward(h, _):
        everything = slice(None)
        dk, dv, dq = back_part(
            h, nkv, everything, nt_kv[feat(h), :], rows,
            lambda s: jnp.where(near_hit(h), s, NEG), lambda p: p,
        )
        accn[:, :width] += dk
        accn[:, width:] += dv
        dk, dv, more = back_part(
            h, pkv, slice(0, half), pt_kv[feat(h), :half], half,
            lambda s: s, lambda p: cp1[...] * p,
        )
        dq = dq + widen(more, 0.0)
        accp[:half, :width] += dk
        accp[:half, width:] += dv
        c2 = cp2[...]
        dk, dv, more = back_part(
            h, pkv, slice(half, None), pt_kv[feat(h), half:], quarter,
            lambda s: jnp.where(c2 > 0.0, s, NEG), lambda p: c2 * p,
        )
        dq = dq + widen(more, 0.0)
        accp[half:, :width] += dk
        accp[half:, width:] += dv
        dqt[feat(h), :] = dq
        return 0

    lax.fori_loop(0, heads, other_backward, 0)
    sendn[...] = accn[...].astype(BF16)
    sendp[...] = accp[...].astype(BF16)
    base = tm + 1
    home = [
        remote(sendn.at[pl.ds(half, half)], gotn.at[pl.ds(0, half)], base, (right, zi)),
        remote(sendn.at[pl.ds(0, half)], gotn.at[pl.ds(half, half)], base + 1, (left, zi)),
    ] + [
        remote(
            sendp.at[pl.ds(slot_of(x), count_of(x))], gotp.at[pl.ds(slot_of(x), count_of(x))],
            base + 1 + x, (flipped(me, x), zi),
        )
        for x in range(1, tm)
    ]
    for copy in home:
        copy.start()

    def own_backward(h, _):
        c = own_count(h)
        dk, dv, dq = back_part(
            h, kvown, slice(None), ownt[feat(h), :], rows,
            lambda s: jnp.where(c > 0.0, s, NEG), lambda p: c * p,
        )
        acco[:, :width] += dk
        acco[:, width:] += dv
        dqt[feat(h), :] += dq
        return 0

    lax.fori_loop(0, heads, own_backward, 0)
    dq_ref[...] = from_order(jnp.transpose(dqt[...]) * scale).astype(BF16)

    for copy in home:
        copy.wait()
    for x in range(1, tm):
        acco[: count_of(x), :] += gotp[slot_of(x) : slot_of(x) + count_of(x), :].astype(F32)
    dkv = from_order(acco[...]) + gotn[...].astype(F32)
    dk_ref[...] = dkv[:, :width].astype(BF16)
    dv_ref[...] = dkv[:, width:].astype(BF16)
    for copy in spread:
        copy.wait()
    for z in range(nz):
        attn_ref[:, z * width : (z + 1) * width] = attng[z]


def on_device(tm, nz, queries, key_states, value_states, out_weight, upstream, windows, offsets):
    rows, width = queries.shape
    heads = windows.shape[0]
    levels = tm.bit_length() - 1
    half, quarter = rows // 2, rows // 4
    peers = levels * half
    vmem = pl.BlockSpec(memory_space=pltpu.VMEM)
    smem = pl.BlockSpec(memory_space=pltpu.SMEM)
    small = jax.ShapeDtypeStruct((rows, width), BF16)
    weight = lax.all_gather(out_weight, "head", axis=0, tiled=True)
    sems = 2 * (tm + 1) + nz
    dq, dk, dv, attn = pl.pallas_call(
        functools.partial(kernel, tm, nz, heads),
        out_shape=(small, small, small, jax.ShapeDtypeStruct((rows, nz * width), BF16)),
        in_specs=[vmem] * 5 + [smem] * 2,
        out_specs=(vmem,) * 4,
        scratch_shapes=[
            pltpu.VMEM((rows, rows), BF16),
            pltpu.VMEM((rows, rows), BF16),
            pltpu.VMEM((heads * rows, width), BF16),
            pltpu.VMEM((heads * rows, width), BF16),
            pltpu.VMEM((width, rows), F32),
            pltpu.VMEM((rows, 2 * width), BF16),
            pltpu.VMEM((rows, 2 * width), BF16),
            pltpu.VMEM((rows, 2 * width), BF16),
            pltpu.VMEM((peers, 2 * width), BF16),
            pltpu.VMEM((2 * width, rows), BF16),
            pltpu.VMEM((2 * width, rows), BF16),
            pltpu.VMEM((2 * width, peers), BF16),
            pltpu.VMEM((rows, rows), F32),
            pltpu.VMEM((half, half), F32),
            pltpu.VMEM((peers - half, quarter), F32),
            pltpu.VMEM((heads, 1, rows), F32),
            pltpu.VMEM((heads, 1, rows), F32),
            pltpu.VMEM((heads, 1, rows), F32),
            pltpu.VMEM((width, rows), F32),
            pltpu.VMEM((width, rows), F32),
            pltpu.VMEM((rows, 2 * width), F32),
            pltpu.VMEM((peers, 2 * width), F32),
            pltpu.VMEM((rows, 2 * width), F32),
            pltpu.VMEM((rows, 2 * width), BF16),
            pltpu.VMEM((peers, 2 * width), BF16),
            pltpu.VMEM((rows, 2 * width), BF16),
            pltpu.VMEM((peers, 2 * width), BF16),
            pltpu.VMEM((nz, rows, width), BF16),
            pltpu.SemaphoreType.DMA((sems,)),
            pltpu.SemaphoreType.DMA((sems,)),
        ],
        compiler_params=pltpu.CompilerParams(
            collective_id=0, has_side_effects=True, vmem_limit_bytes=50 * 2**20
        ),
        cost_estimate=pl.CostEstimate(
            flops=20 * 10**9, bytes_accessed=6 * 2**20, transcendentals=6 * 10**6
        ),
    )(queries, key_states, value_states, out_weight, upstream, windows, offsets)
    mixed = jnp.dot(attn, weight, preferred_element_type=F32).astype(BF16)
    return mixed, dq, dk, dv


def solution(mesh):
    placed = (
        P("tm", "head"),
        P("tm", "head"),
        P("tm", "head"),
        P("head", None),
        P("tm", None),
        P("head"),
        P("head"),
    )
    return jax.shard_map(
        functools.partial(on_device, mesh.shape["tm"], mesh.shape["head"]),
        mesh=mesh,
        in_specs=placed,
        out_specs=(P("tm", None), P("tm", "head"), P("tm", "head"), P("tm", "head")),
        check_vma=False,
    )
```

```python
import functools
import math

import jax
import jax.numpy as jnp
from jax import lax
from jax.experimental import pallas as pl
from jax.experimental.pallas import tpu as pltpu
from jax.sharding import PartitionSpec as P

MESH = pl.DeviceIdType.MESH
F32 = jnp.float32
BF16 = jnp.bfloat16
NEG = -1e30


def nt(a, b):
    return lax.dot_general(a, b, (((1,), (1,)), ((), ())), preferred_element_type=F32)


def nn(a, b):
    return lax.dot_general(a, b, (((1,), (0,)), ((), ())), preferred_element_type=F32)


def flipped(me, x):
    peer = me
    for k in range(x.bit_length()):
        if x >> k & 1:
            peer = peer + (1 - 2 * (me // 2**k % 2)) * 2**k
    return peer


def kernel(
    tm, nz, heads,
    q_in, k_in, v_in, w_in, up_in, win_ref, off_ref,
    mixed_ref, dq_ref, dk_ref, dv_ref,
    q_ref, up_ref, weights,
    order, back, q4, g4, gt, kvnat, kvown, nkv, pkv, ownt, nt_kv, pt_kv,
    cown, cp1, cp2, top, total, delta, ot, dqt,
    accn, accp, acco, sendn, sendp, gotn, gotp, attng, load_sem, send_sem, recv_sem,
):
    rows, width = q_in.shape
    dim = width // heads
    levels = tm.bit_length() - 1
    half = rows // 2
    slab = rows // tm
    quarter = rows // 4
    scale = 1.0 / math.sqrt(dim)
    me = lax.axis_index("tm")
    zi = lax.axis_index("head")
    loads = [
        pltpu.make_async_copy(src, dst, load_sem.at[i])
        for i, (src, dst) in enumerate(
            [
                (k_in, kvnat.at[:, pl.ds(0, width)]),
                (v_in, kvnat.at[:, pl.ds(width, width)]),
                (w_in, weights.at[zi]),
                (q_in, q_ref),
                (up_in, up_ref),
            ]
        )
    ]
    for load in loads:
        load.start()
    right = (me + 1) % tm
    left = (me + tm - 1) % tm

    barrier = pltpu.get_barrier_semaphore()
    for x in range(1, tm):
        pl.semaphore_signal(
            barrier, inc=1, device_id=((me + x) % tm, zi), device_id_type=MESH
        )
    for x in range(1, nz):
        pl.semaphore_signal(
            barrier, inc=1, device_id=(me, (zi + x) % nz), device_id_type=MESH
        )

    def count_of(x):
        return rows >> x.bit_length()

    def slot_of(x):
        m = x.bit_length()
        return (m - 1) * half + (x - 2 ** (m - 1)) * (rows >> m)

    def remote(src, dst, sem, device):
        return pltpu.make_async_remote_copy(
            src_ref=src, dst_ref=dst, send_sem=send_sem.at[sem], recv_sem=recv_sem.at[sem],
            device_id=device, device_id_type=MESH,
        )

    pl.semaphore_wait(barrier, tm + nz - 2)
    loads[0].wait()
    loads[1].wait()
    near = [
        remote(kvnat.at[pl.ds(half, half)], nkv.at[pl.ds(0, half)], 0, (right, zi)),
        remote(kvnat.at[pl.ds(0, half)], nkv.at[pl.ds(half, half)], 1, (left, zi)),
    ]
    for copy in near:
        copy.start()

    def reversed_bits(s):
        out = jnp.zeros_like(s)
        for k in range(levels):
            out = out + ((s >> k) & 1) * 2 ** (levels - 1 - k)
        return out

    def place(row):
        return (row % slab) * tm + reversed_bits(row // slab)

    iota = lambda shape, axis: lax.broadcasted_iota(jnp.int32, shape, axis)
    place_col = place(iota((rows, 1), 0))
    place_row = place(iota((1, rows), 1))
    order[...] = jnp.where(iota((rows, rows), 1) == place_col, 1.0, 0.0).astype(BF16)
    back[...] = jnp.where(iota((rows, rows), 0) == place_row, 1.0, 0.0).astype(BF16)

    def off_cols(cols):
        head = (iota((1, cols), 1) % width) // dim
        out = jnp.zeros((1, cols), jnp.int32)
        for h in range(heads):
            out = jnp.where(head == h, off_ref[h], out)
        return out

    def swapped(x):
        off = off_cols(x.shape[1])
        for k in range(levels):
            size = slab * 2 ** (levels - 1 - k)
            other = jnp.concatenate(
                [x[(i ^ 1) * size : (i ^ 1) * size + size] for i in range(rows // size)], 0
            )
            x = jnp.where(((off >> k) & 1) == 1, other, x)
        return x

    def to_order(x):
        return swapped(nn(order[...], x))

    def from_order(x):
        return nn(back[...], swapped(x).astype(BF16))

    part = pl.ds(pl.multiple_of((me % 2) * (width // 2), width // 2), width // 2)
    loads[2].wait()
    wide = [
        remote(
            weights.at[zi, part], weights.at[zi, part], 2 * tm + 1 + nz + x,
            (me, (zi + x) % nz),
        )
        for x in range(1, nz)
    ]
    kvp = to_order(kvnat[...])
    kvown[...] = kvp.astype(BF16)
    far = [
        remote(
            kvown.at[pl.ds(0, count_of(x))], pkv.at[pl.ds(slot_of(x), count_of(x))], 1 + x,
            (flipped(me, x), zi),
        )
        for x in range(1, tm)
    ]
    for copy in far + wide:
        copy.start()
    loads[3].wait()
    loads[4].wait()
    ownt[...] = jnp.transpose(kvp).astype(BF16)
    col_head = iota((1, width), 1) // dim
    qp = to_order(q_ref[...]) * scale
    grad = nt(up_ref[...], weights[zi]).astype(BF16)
    gp = to_order(grad)
    gt[...] = jnp.transpose(gp)
    for h in range(heads):
        at = pl.ds(h * rows, rows)
        q4[at, :] = jnp.where(col_head == h, qp, 0.0).astype(BF16)
        g4[at, :] = jnp.where(col_head == h, gp, 0.0).astype(BF16)

    def shared(i, j, first):
        out = jnp.zeros(jnp.broadcast_shapes(i.shape, j.shape), F32)
        for l in range(first, levels + 1):
            out = out + jnp.where(jnp.maximum(i, j) < (rows >> l), 1.0, 0.0)
        return out

    cown[...] = shared(iota((1, rows), 1), iota((rows, 1), 0), 1)
    cp1[...] = shared(iota((1, half), 1), iota((half, 1), 0), 1)
    for m in range(2, levels + 1):
        cp2[pl.ds((m - 2) * half, half), :] = shared(
            iota((1, quarter), 1), iota((half, 1), 0) % (rows >> m), m
        )

    near_row = iota((rows, 1), 0)
    gap = 8 * rows
    pos_near = jnp.where(
        near_row < half,
        jnp.where(me > 0, near_row - half, -gap),
        jnp.where(me < tm - 1, near_row + half, gap),
    )

    def own_count(h):
        off = off_ref[h] % tm
        d = (place_col ^ off) - (place_row ^ off)
        return cown[...] + jnp.where(jnp.abs(d) <= win_ref[h], 1.0, 0.0)

    def near_hit(h):
        off = off_ref[h] % tm
        return jnp.abs(pos_near - (place_row ^ off)) <= win_ref[h]

    def sum0(x):
        return jnp.sum(x, axis=0, keepdims=True)

    def max0(x):
        return jnp.max(x, axis=0, keepdims=True)

    def head_rows(h, count):
        return pl.ds(pl.multiple_of(h * rows, rows), count)

    def feat(h):
        return pl.ds(pl.multiple_of(h * dim, dim), dim)

    def vfeat(h):
        return pl.ds(pl.multiple_of(width + h * dim, dim), dim)

    def own_forward(h, _):
        s = nt(kvown[:, :width], q4[head_rows(h, rows), :])
        c = own_count(h)
        s = jnp.where(c > 0.0, s, NEG)
        m = max0(s)
        p = c * jnp.exp(s - m)
        top[h] = m
        total[h] = sum0(p)
        ot[feat(h), :] = nn(ownt[vfeat(h), :], p.astype(BF16))
        return 0

    lax.fori_loop(0, heads, own_forward, 0)

    for copy in near + far:
        copy.wait()
    nt_kv[...] = jnp.transpose(nkv[...].astype(F32)).astype(BF16)
    pt_kv[...] = jnp.transpose(pkv[...].astype(F32)).astype(BF16)

    def widen(a, fill):
        missing = rows - a.shape[1]
        return jnp.concatenate([a, jnp.full((a.shape[0], missing), fill, F32)], 1)

    def other_forward(h, _):
        sn = nt(nkv[:, :width], q4[head_rows(h, rows), :])
        s1 = nt(pkv[:half, :width], q4[head_rows(h, half), :])
        s2 = nt(pkv[half:, :width], q4[head_rows(h, quarter), :])
        sn = jnp.where(near_hit(h), sn, NEG)
        c2 = cp2[...]
        s2 = jnp.where(c2 > 0.0, s2, NEG)
        m0 = top[h]
        m = jnp.maximum(
            jnp.maximum(m0, max0(sn)),
            jnp.maximum(widen(max0(s1), NEG), widen(max0(s2), NEG)),
        )
        pn = jnp.exp(sn - m)
        p1 = cp1[...] * jnp.exp(s1 - m[:, :half])
        p2 = c2 * jnp.exp(s2 - m[:, :quarter])
        keep = jnp.exp(m0 - m)
        l = total[h] * keep + sum0(pn) + widen(sum0(p1), 0.0) + widen(sum0(p2), 0.0)
        o = ot[feat(h), :] * keep + nn(nt_kv[vfeat(h), :], pn.astype(BF16))
        o = o + widen(nn(pt_kv[vfeat(h), :half], p1.astype(BF16)), 0.0)
        o = o + widen(nn(pt_kv[vfeat(h), half:], p2.astype(BF16)), 0.0)
        o = (o / l).astype(BF16).astype(F32)
        ot[feat(h), :] = o
        top[h] = m + jnp.log(l)
        delta[h] = sum0(o * gt[feat(h), :])
        return 0

    lax.fori_loop(0, heads, other_forward, 0)

    attng[zi] = from_order(jnp.transpose(ot[...])).astype(BF16)
    spread = [
        remote(attng.at[zi], attng.at[zi], 2 * tm + 1 + x, (me, (zi + x) % nz))
        for x in range(1, nz)
    ]
    for copy in spread:
        copy.start()

    accn[...] = jnp.zeros_like(accn)
    accp[...] = jnp.zeros_like(accp)
    acco[...] = jnp.zeros_like(acco)

    def back_part(h, kv, at, kt, queries, s_of, c_of):
        q = q4[head_rows(h, queries), :]
        g = g4[head_rows(h, queries), :]
        s = s_of(nt(kv[at, :width], q))
        p = jnp.exp(s - top[h][:, :queries])
        p = c_of(p)
        dots = nt(kv[at, width:], g)
        ds = (p * (dots - delta[h][:, :queries])).astype(BF16)
        return nn(ds, q), nn(p.astype(BF16), g), nn(kt, ds)

    def other_backward(h, _):
        everything = slice(None)
        dk, dv, dq = back_part(
            h, nkv, everything, nt_kv[feat(h), :], rows,
            lambda s: jnp.where(near_hit(h), s, NEG), lambda p: p,
        )
        accn[:, :width] += dk
        accn[:, width:] += dv
        dk, dv, more = back_part(
            h, pkv, slice(0, half), pt_kv[feat(h), :half], half,
            lambda s: s, lambda p: cp1[...] * p,
        )
        dq = dq + widen(more, 0.0)
        accp[:half, :width] += dk
        accp[:half, width:] += dv
        c2 = cp2[...]
        dk, dv, more = back_part(
            h, pkv, slice(half, None), pt_kv[feat(h), half:], quarter,
            lambda s: jnp.where(c2 > 0.0, s, NEG), lambda p: c2 * p,
        )
        dq = dq + widen(more, 0.0)
        accp[half:, :width] += dk
        accp[half:, width:] += dv
        dqt[feat(h), :] = dq
        return 0

    lax.fori_loop(0, heads, other_backward, 0)
    for copy in wide:
        copy.wait()
    twin = []
    for x in range(1, nz):
        z = (zi + nz - x) % nz
        twin.append(
            remote(
                weights.at[z, part], weights.at[z, part], 2 * tm + 1 + 2 * nz + x,
                (flipped(me, 1), zi),
            )
        )
        twin[-1].start()
    sendn[...] = accn[...].astype(BF16)
    sendp[...] = accp[...].astype(BF16)
    base = tm + 1
    home = [
        remote(sendn.at[pl.ds(half, half)], gotn.at[pl.ds(0, half)], base, (right, zi)),
        remote(sendn.at[pl.ds(0, half)], gotn.at[pl.ds(half, half)], base + 1, (left, zi)),
    ] + [
        remote(
            sendp.at[pl.ds(slot_of(x), count_of(x))], gotp.at[pl.ds(slot_of(x), count_of(x))],
            base + 1 + x, (flipped(me, x), zi),
        )
        for x in range(1, tm)
    ]
    for copy in home:
        copy.start()

    def own_backward(h, _):
        c = own_count(h)
        dk, dv, dq = back_part(
            h, kvown, slice(None), ownt[feat(h), :], rows,
            lambda s: jnp.where(c > 0.0, s, NEG), lambda p: c * p,
        )
        acco[:, :width] += dk
        acco[:, width:] += dv
        dqt[feat(h), :] += dq
        return 0

    lax.fori_loop(0, heads, own_backward, 0)
    dq_ref[...] = from_order(jnp.transpose(dqt[...]) * scale).astype(BF16)

    for copy in spread + twin:
        copy.wait()
    mixed = nn(attng[0], weights[0])
    for z in range(1, nz):
        mixed = mixed + nn(attng[z], weights[z])
    mixed_ref[...] = mixed.astype(BF16)
    for copy in home:
        copy.wait()
    for x in range(1, tm):
        acco[: count_of(x), :] += gotp[slot_of(x) : slot_of(x) + count_of(x), :].astype(F32)
    dkv = from_order(acco[...]) + gotn[...].astype(F32)
    dk_ref[...] = dkv[:, :width].astype(BF16)
    dv_ref[...] = dkv[:, width:].astype(BF16)


def on_device(tm, nz, queries, key_states, value_states, out_weight, upstream, windows, offsets):
    rows, width = queries.shape
    heads = windows.shape[0]
    levels = tm.bit_length() - 1
    half, quarter = rows // 2, rows // 4
    peers = levels * half
    vmem = pl.BlockSpec(memory_space=pltpu.VMEM)
    smem = pl.BlockSpec(memory_space=pltpu.SMEM)
    small = jax.ShapeDtypeStruct((rows, width), BF16)
    model = out_weight.shape[1]
    hbm = pl.BlockSpec(memory_space=pltpu.HBM)
    sems = 2 * (tm + 1) + 3 * nz
    return pl.pallas_call(
        functools.partial(kernel, tm, nz, heads),
        out_shape=(jax.ShapeDtypeStruct((rows, model), BF16), small, small, small),
        in_specs=[hbm] * 5 + [smem] * 2,
        out_specs=(vmem,) * 4,
        scratch_shapes=[
            pltpu.VMEM((rows, width), BF16),
            pltpu.VMEM((rows, model), BF16),
            pltpu.VMEM((nz, width, model), BF16),
            pltpu.VMEM((rows, rows), BF16),
            pltpu.VMEM((rows, rows), BF16),
            pltpu.VMEM((heads * rows, width), BF16),
            pltpu.VMEM((heads * rows, width), BF16),
            pltpu.VMEM((width, rows), F32),
            pltpu.VMEM((rows, 2 * width), BF16),
            pltpu.VMEM((rows, 2 * width), BF16),
            pltpu.VMEM((rows, 2 * width), BF16),
            pltpu.VMEM((peers, 2 * width), BF16),
            pltpu.VMEM((2 * width, rows), BF16),
            pltpu.VMEM((2 * width, rows), BF16),
            pltpu.VMEM((2 * width, peers), BF16),
            pltpu.VMEM((rows, rows), F32),
            pltpu.VMEM((half, half), F32),
            pltpu.VMEM((peers - half, quarter), F32),
            pltpu.VMEM((heads, 1, rows), F32),
            pltpu.VMEM((heads, 1, rows), F32),
            pltpu.VMEM((heads, 1, rows), F32),
            pltpu.VMEM((width, rows), F32),
            pltpu.VMEM((width, rows), F32),
            pltpu.VMEM((rows, 2 * width), F32),
            pltpu.VMEM((peers, 2 * width), F32),
            pltpu.VMEM((rows, 2 * width), F32),
            pltpu.VMEM((rows, 2 * width), BF16),
            pltpu.VMEM((peers, 2 * width), BF16),
            pltpu.VMEM((rows, 2 * width), BF16),
            pltpu.VMEM((peers, 2 * width), BF16),
            pltpu.VMEM((nz, rows, width), BF16),
            pltpu.SemaphoreType.DMA((5,)),
            pltpu.SemaphoreType.DMA((sems,)),
            pltpu.SemaphoreType.DMA((sems,)),
        ],
        compiler_params=pltpu.CompilerParams(
            collective_id=0, has_side_effects=True, vmem_limit_bytes=60 * 2**20
        ),
        cost_estimate=pl.CostEstimate(
            flops=20 * 10**9, bytes_accessed=6 * 2**20, transcendentals=6 * 10**6
        ),
    )(queries, key_states, value_states, out_weight, upstream, windows, offsets)


def solution(mesh):
    placed = (
        P("tm", "head"),
        P("tm", "head"),
        P("tm", "head"),
        P("head", None),
        P("tm", None),
        P("head"),
        P("head"),
    )
    return jax.shard_map(
        functools.partial(on_device, mesh.shape["tm"], mesh.shape["head"]),
        mesh=mesh,
        in_specs=placed,
        out_specs=(P("tm", None), P("tm", "head"), P("tm", "head"), P("tm", "head")),
        check_vma=False,
    )
```

```python
import functools
import math

import jax
import jax.numpy as jnp
from jax import lax
from jax.experimental import pallas as pl
from jax.experimental.pallas import tpu as pltpu
from jax.sharding import PartitionSpec as P

MESH = pl.DeviceIdType.MESH
F32 = jnp.float32
BF16 = jnp.bfloat16
NEG = -1e30


def nt(a, b):
    return lax.dot_general(a, b, (((1,), (1,)), ((), ())), preferred_element_type=F32)


def nn(a, b):
    return lax.dot_general(a, b, (((1,), (0,)), ((), ())), preferred_element_type=F32)


def flipped(me, x):
    peer = me
    for k in range(x.bit_length()):
        if x >> k & 1:
            peer = peer + (1 - 2 * (me // 2**k % 2)) * 2**k
    return peer


def kernel(
    tm, nz, heads,
    q_in, k_in, v_in, w_in, up_in, win_ref, off_ref,
    mixed_ref, dq_ref, dk_ref, dv_ref,
    q_ref, up_ref, weights,
    order, back, q4, g4, gt, kvnat, kvown, nkv, pkv, ownt, nt_kv, pt_kv,
    cown, cp1, cp2, top, total, delta, ot, dqt,
    accn, accp, acco, sendn, sendp, gotn, gotp, attng, load_sem, send_sem, recv_sem,
):
    rows, width = q_in.shape
    dim = width // heads
    levels = tm.bit_length() - 1
    half = rows // 2
    slab = rows // tm
    quarter = rows // 4
    scale = 1.0 / math.sqrt(dim)
    me = lax.axis_index("tm")
    zi = lax.axis_index("head")
    loads = [
        pltpu.make_async_copy(src, dst, load_sem.at[i])
        for i, (src, dst) in enumerate(
            [
                (k_in, kvnat.at[:, pl.ds(0, width)]),
                (v_in, kvnat.at[:, pl.ds(width, width)]),
                (w_in, weights.at[zi]),
                (q_in, q_ref),
                (up_in, up_ref),
            ]
        )
    ]
    for load in loads:
        load.start()
    right = (me + 1) % tm
    left = (me + tm - 1) % tm

    barrier = pltpu.get_barrier_semaphore()
    for x in range(1, tm):
        pl.semaphore_signal(
            barrier, inc=1, device_id=((me + x) % tm, zi), device_id_type=MESH
        )
    for x in range(1, nz):
        pl.semaphore_signal(
            barrier, inc=1, device_id=(me, (zi + x) % nz), device_id_type=MESH
        )

    def count_of(x):
        return rows >> x.bit_length()

    def slot_of(x):
        m = x.bit_length()
        return (m - 1) * half + (x - 2 ** (m - 1)) * (rows >> m)

    def remote(src, dst, sem, device):
        return pltpu.make_async_remote_copy(
            src_ref=src, dst_ref=dst, send_sem=send_sem.at[sem], recv_sem=recv_sem.at[sem],
            device_id=device, device_id_type=MESH,
        )

    pl.semaphore_wait(barrier, tm + nz - 2)
    loads[0].wait()
    loads[1].wait()
    near = [
        remote(kvnat.at[pl.ds(half, half)], nkv.at[pl.ds(0, half)], 0, (right, zi)),
        remote(kvnat.at[pl.ds(0, half)], nkv.at[pl.ds(half, half)], 1, (left, zi)),
    ]
    for copy in near:
        copy.start()

    def reversed_bits(s):
        out = jnp.zeros_like(s)
        for k in range(levels):
            out = out + ((s >> k) & 1) * 2 ** (levels - 1 - k)
        return out

    def place(row):
        return (row % slab) * tm + reversed_bits(row // slab)

    iota = lambda shape, axis: lax.broadcasted_iota(jnp.int32, shape, axis)
    place_col = place(iota((rows, 1), 0))
    place_row = place(iota((1, rows), 1))
    order[...] = jnp.where(iota((rows, rows), 1) == place_col, 1.0, 0.0).astype(BF16)
    back[...] = jnp.where(iota((rows, rows), 0) == place_row, 1.0, 0.0).astype(BF16)

    def off_cols(cols):
        head = (iota((1, cols), 1) % width) // dim
        out = jnp.zeros((1, cols), jnp.int32)
        for h in range(heads):
            out = jnp.where(head == h, off_ref[h], out)
        return out

    def swapped(x):
        off = off_cols(x.shape[1])
        for k in range(levels):
            size = slab * 2 ** (levels - 1 - k)
            other = jnp.concatenate(
                [x[(i ^ 1) * size : (i ^ 1) * size + size] for i in range(rows // size)], 0
            )
            x = jnp.where(((off >> k) & 1) == 1, other, x)
        return x

    def to_order(x):
        return swapped(nn(order[...], x))

    def from_order(x):
        return nn(back[...], swapped(x).astype(BF16))

    part = pl.ds(pl.multiple_of((me % 2) * (width // 2), width // 2), width // 2)
    loads[2].wait()
    wide = [
        remote(
            weights.at[zi, part], weights.at[zi, part], 2 * tm + 1 + nz + x,
            (me, (zi + x) % nz),
        )
        for x in range(1, nz)
    ]
    kvp = to_order(kvnat[...])
    kvown[...] = kvp.astype(BF16)
    far = [
        remote(
            kvown.at[pl.ds(0, count_of(x))], pkv.at[pl.ds(slot_of(x), count_of(x))], 1 + x,
            (flipped(me, x), zi),
        )
        for x in range(1, tm)
    ]
    for copy in far + wide:
        copy.start()
    loads[3].wait()
    loads[4].wait()
    ownt[...] = jnp.transpose(kvp).astype(BF16)
    col_head = iota((1, width), 1) // dim
    qp = to_order(q_ref[...]) * scale
    grad = nt(up_ref[...], weights[zi]).astype(BF16)
    gp = to_order(grad)
    gt[...] = jnp.transpose(gp)
    for h in range(heads):
        at = pl.ds(h * rows, rows)
        q4[at, :] = jnp.where(col_head == h, qp, 0.0).astype(BF16)
        g4[at, :] = jnp.where(col_head == h, gp, 0.0).astype(BF16)

    def shared(i, j, first):
        out = jnp.zeros(jnp.broadcast_shapes(i.shape, j.shape), F32)
        for l in range(first, levels + 1):
            out = out + jnp.where(jnp.maximum(i, j) < (rows >> l), 1.0, 0.0)
        return out

    cown[...] = shared(iota((1, rows), 1), iota((rows, 1), 0), 1)
    cp1[...] = shared(iota((1, half), 1), iota((half, 1), 0), 1)
    for m in range(2, levels + 1):
        cp2[pl.ds((m - 2) * half, half), :] = shared(
            iota((1, quarter), 1), iota((half, 1), 0) % (rows >> m), m
        )

    near_row = iota((rows, 1), 0)
    gap = 8 * rows
    pos_near = jnp.where(
        near_row < half,
        jnp.where(me > 0, near_row - half, -gap),
        jnp.where(me < tm - 1, near_row + half, gap),
    )

    def own_count(h):
        off = off_ref[h] % tm
        d = (place_col ^ off) - (place_row ^ off)
        return cown[...] + jnp.where(jnp.abs(d) <= win_ref[h], 1.0, 0.0)

    def near_hit(h):
        off = off_ref[h] % tm
        return jnp.abs(pos_near - (place_row ^ off)) <= win_ref[h]

    def sum0(x):
        return jnp.sum(x, axis=0, keepdims=True)

    def max0(x):
        return jnp.max(x, axis=0, keepdims=True)

    def head_rows(h, count):
        return pl.ds(pl.multiple_of(h * rows, rows), count)

    def feat(h):
        return pl.ds(pl.multiple_of(h * dim, dim), dim)

    def vfeat(h):
        return pl.ds(pl.multiple_of(width + h * dim, dim), dim)

    def own_forward(h, _):
        s = nt(kvown[:, :width], q4[head_rows(h, rows), :])
        c = own_count(h)
        s = jnp.where(c > 0.0, s, NEG)
        m = max0(s)
        p = c * jnp.exp(s - m)
        top[h] = m
        total[h] = sum0(p)
        ot[feat(h), :] = nn(ownt[vfeat(h), :], p.astype(BF16))
        return 0

    lax.fori_loop(0, heads, own_forward, 0)

    for copy in near + far:
        copy.wait()
    nt_kv[...] = jnp.transpose(nkv[...].astype(F32)).astype(BF16)
    pt_kv[...] = jnp.transpose(pkv[...].astype(F32)).astype(BF16)

    def widen(a, fill):
        missing = rows - a.shape[1]
        return jnp.concatenate([a, jnp.full((a.shape[0], missing), fill, F32)], 1)

    def other_forward(h, _):
        sn = nt(nkv[:, :width], q4[head_rows(h, rows), :])
        s1 = nt(pkv[:half, :width], q4[head_rows(h, half), :])
        s2 = nt(pkv[half:, :width], q4[head_rows(h, quarter), :])
        sn = jnp.where(near_hit(h), sn, NEG)
        c2 = cp2[...]
        s2 = jnp.where(c2 > 0.0, s2, NEG)
        m0 = top[h]
        m = jnp.maximum(
            jnp.maximum(m0, max0(sn)),
            jnp.maximum(widen(max0(s1), NEG), widen(max0(s2), NEG)),
        )
        pn = jnp.exp(sn - m)
        p1 = cp1[...] * jnp.exp(s1 - m[:, :half])
        p2 = c2 * jnp.exp(s2 - m[:, :quarter])
        keep = jnp.exp(m0 - m)
        l = total[h] * keep + sum0(pn) + widen(sum0(p1), 0.0) + widen(sum0(p2), 0.0)
        o = ot[feat(h), :] * keep + nn(nt_kv[vfeat(h), :], pn.astype(BF16))
        o = o + widen(nn(pt_kv[vfeat(h), :half], p1.astype(BF16)), 0.0)
        o = o + widen(nn(pt_kv[vfeat(h), half:], p2.astype(BF16)), 0.0)
        o = (o / l).astype(BF16).astype(F32)
        ot[feat(h), :] = o
        top[h] = m + jnp.log(l)
        delta[h] = sum0(o * gt[feat(h), :])
        return 0

    lax.fori_loop(0, heads, other_forward, 0)

    attng[zi] = from_order(jnp.transpose(ot[...])).astype(BF16)
    def hop(step, up):
        block = (zi - step + 1 + nz) % nz if up else (zi + step - 1) % nz
        peer = (zi + 1) % nz if up else (zi + nz - 1) % nz
        sem = 2 * tm + 1 + step + (0 if up else 3 * nz)
        holds = zi >= step - 1 if up else zi <= nz - step
        gets = zi >= step if up else zi < nz - step
        sends = jnp.logical_and(holds, zi < nz - 1 if up else zi > 0)
        return remote(attng.at[block], attng.at[block], sem, (me, peer)), sends, gets

    def hop_start(step):
        for up in (True, False):
            copy, sends, _ = hop(step, up)
            pl.when(sends)(copy.start)

    def hop_wait(step):
        for up in (True, False):
            copy, sends, gets = hop(step, up)
            pl.when(sends)(copy.wait_send)
            pl.when(gets)(copy.wait_recv)

    hop_start(1)

    accn[...] = jnp.zeros_like(accn)
    accp[...] = jnp.zeros_like(accp)
    acco[...] = jnp.zeros_like(acco)

    def back_part(h, kv, at, kt, queries, s_of, c_of):
        q = q4[head_rows(h, queries), :]
        g = g4[head_rows(h, queries), :]
        s = s_of(nt(kv[at, :width], q))
        p = jnp.exp(s - top[h][:, :queries])
        p = c_of(p)
        dots = nt(kv[at, width:], g)
        ds = (p * (dots - delta[h][:, :queries])).astype(BF16)
        return nn(ds, q), nn(p.astype(BF16), g), nn(kt, ds)

    def other_backward(h, _):
        everything = slice(None)
        dk, dv, dq = back_part(
            h, nkv, everything, nt_kv[feat(h), :], rows,
            lambda s: jnp.where(near_hit(h), s, NEG), lambda p: p,
        )
        accn[:, :width] += dk
        accn[:, width:] += dv
        dk, dv, more = back_part(
            h, pkv, slice(0, half), pt_kv[feat(h), :half], half,
            lambda s: s, lambda p: cp1[...] * p,
        )
        dq = dq + widen(more, 0.0)
        accp[:half, :width] += dk
        accp[:half, width:] += dv
        c2 = cp2[...]
        dk, dv, more = back_part(
            h, pkv, slice(half, None), pt_kv[feat(h), half:], quarter,
            lambda s: jnp.where(c2 > 0.0, s, NEG), lambda p: c2 * p,
        )
        dq = dq + widen(more, 0.0)
        accp[half:, :width] += dk
        accp[half:, width:] += dv
        dqt[feat(h), :] = dq
        return 0

    lax.fori_loop(0, heads, other_backward, 0)
    hop_wait(1)
    hop_start(2)
    for copy in wide:
        copy.wait()
    twin = []
    for x in range(1, nz):
        z = (zi + nz - x) % nz
        twin.append(
            remote(
                weights.at[z, part], weights.at[z, part], 2 * tm + 1 + 2 * nz + x,
                (flipped(me, 1), zi),
            )
        )
        twin[-1].start()
    sendn[...] = accn[...].astype(BF16)
    sendp[...] = accp[...].astype(BF16)
    base = tm + 1
    home = [
        remote(sendn.at[pl.ds(half, half)], gotn.at[pl.ds(0, half)], base, (right, zi)),
        remote(sendn.at[pl.ds(0, half)], gotn.at[pl.ds(half, half)], base + 1, (left, zi)),
    ] + [
        remote(
            sendp.at[pl.ds(slot_of(x), count_of(x))], gotp.at[pl.ds(slot_of(x), count_of(x))],
            base + 1 + x, (flipped(me, x), zi),
        )
        for x in range(1, tm)
    ]
    for copy in home:
        copy.start()

    def own_backward(h, _):
        c = own_count(h)
        dk, dv, dq = back_part(
            h, kvown, slice(None), ownt[feat(h), :], rows,
            lambda s: jnp.where(c > 0.0, s, NEG), lambda p: c * p,
        )
        acco[:, :width] += dk
        acco[:, width:] += dv
        dqt[feat(h), :] += dq
        return 0

    lax.fori_loop(0, heads, own_backward, 0)
    dq_ref[...] = from_order(jnp.transpose(dqt[...]) * scale).astype(BF16)

    for step in range(2, nz):
        hop_wait(step)
        if step < nz - 1:
            hop_start(step + 1)
    for copy in twin:
        copy.wait()
    mixed = nn(attng[0], weights[0])
    for z in range(1, nz):
        mixed = mixed + nn(attng[z], weights[z])
    mixed_ref[...] = mixed.astype(BF16)
    for copy in home:
        copy.wait()
    for x in range(1, tm):
        acco[: count_of(x), :] += gotp[slot_of(x) : slot_of(x) + count_of(x), :].astype(F32)
    dkv = from_order(acco[...]) + gotn[...].astype(F32)
    dk_ref[...] = dkv[:, :width].astype(BF16)
    dv_ref[...] = dkv[:, width:].astype(BF16)


def on_device(tm, nz, queries, key_states, value_states, out_weight, upstream, windows, offsets):
    rows, width = queries.shape
    heads = windows.shape[0]
    levels = tm.bit_length() - 1
    half, quarter = rows // 2, rows // 4
    peers = levels * half
    vmem = pl.BlockSpec(memory_space=pltpu.VMEM)
    smem = pl.BlockSpec(memory_space=pltpu.SMEM)
    small = jax.ShapeDtypeStruct((rows, width), BF16)
    model = out_weight.shape[1]
    hbm = pl.BlockSpec(memory_space=pltpu.HBM)
    sems = 2 * (tm + 1) + 4 * nz
    return pl.pallas_call(
        functools.partial(kernel, tm, nz, heads),
        out_shape=(jax.ShapeDtypeStruct((rows, model), BF16), small, small, small),
        in_specs=[hbm] * 5 + [smem] * 2,
        out_specs=(vmem,) * 4,
        scratch_shapes=[
            pltpu.VMEM((rows, width), BF16),
            pltpu.VMEM((rows, model), BF16),
            pltpu.VMEM((nz, width, model), BF16),
            pltpu.VMEM((rows, rows), BF16),
            pltpu.VMEM((rows, rows), BF16),
            pltpu.VMEM((heads * rows, width), BF16),
            pltpu.VMEM((heads * rows, width), BF16),
            pltpu.VMEM((width, rows), F32),
            pltpu.VMEM((rows, 2 * width), BF16),
            pltpu.VMEM((rows, 2 * width), BF16),
            pltpu.VMEM((rows, 2 * width), BF16),
            pltpu.VMEM((peers, 2 * width), BF16),
            pltpu.VMEM((2 * width, rows), BF16),
            pltpu.VMEM((2 * width, rows), BF16),
            pltpu.VMEM((2 * width, peers), BF16),
            pltpu.VMEM((rows, rows), F32),
            pltpu.VMEM((half, half), F32),
            pltpu.VMEM((peers - half, quarter), F32),
            pltpu.VMEM((heads, 1, rows), F32),
            pltpu.VMEM((heads, 1, rows), F32),
            pltpu.VMEM((heads, 1, rows), F32),
            pltpu.VMEM((width, rows), F32),
            pltpu.VMEM((width, rows), F32),
            pltpu.VMEM((rows, 2 * width), F32),
            pltpu.VMEM((peers, 2 * width), F32),
            pltpu.VMEM((rows, 2 * width), F32),
            pltpu.VMEM((rows, 2 * width), BF16),
            pltpu.VMEM((peers, 2 * width), BF16),
            pltpu.VMEM((rows, 2 * width), BF16),
            pltpu.VMEM((peers, 2 * width), BF16),
            pltpu.VMEM((nz, rows, width), BF16),
            pltpu.SemaphoreType.DMA((5,)),
            pltpu.SemaphoreType.DMA((sems,)),
            pltpu.SemaphoreType.DMA((sems,)),
        ],
        compiler_params=pltpu.CompilerParams(
            collective_id=0, has_side_effects=True, vmem_limit_bytes=60 * 2**20
        ),
        cost_estimate=pl.CostEstimate(
            flops=20 * 10**9, bytes_accessed=6 * 2**20, transcendentals=6 * 10**6
        ),
    )(queries, key_states, value_states, out_weight, upstream, windows, offsets)


def solution(mesh):
    placed = (
        P("tm", "head"),
        P("tm", "head"),
        P("tm", "head"),
        P("head", None),
        P("tm", None),
        P("head"),
        P("head"),
    )
    return jax.shard_map(
        functools.partial(on_device, mesh.shape["tm"], mesh.shape["head"]),
        mesh=mesh,
        in_specs=placed,
        out_specs=(P("tm", None), P("tm", "head"), P("tm", "head"), P("tm", "head")),
        check_vma=False,
    )
```
